32 devices in a mesh: grp: 2 (over y), dev: 4 (over z), tp: 4 (over x, core).
Axes of the slice: x: 2, y: 2, z: 4, core: 2. Of those that a mesh axis runs over, the one named last changes fastest.
Arguments:
- passage_hidden: bfloat16 [8192, 3584], P(('grp', 'dev', 'tp')), parts along dimension 0, may hold values from -6 to 6
- query_hidden: bfloat16 [1024, 3584], P(('grp', 'dev', 'tp')), parts along dimension 0, may hold values from -6 to 6
- gain_in: bfloat16 [3584], replicated, may hold values from 0.5 to 1.5
- gain_out: bfloat16 [3584], replicated, may hold values from 0.5 to 1.5
- w_query: bfloat16 [3584, 4096], P(None, 'tp'), may hold values from -2 to 2
- w_key: bfloat16 [3584, 2048], P(None, 'tp'), may hold values from -2 to 2
- w_value: bfloat16 [3584, 2048], P(None, 'tp'), may hold values from -0.09375 to 0.09375
- w_out: bfloat16 [4096, 3584], P('tp'), may hold values from -0.09375 to 0.09375
- pair_passage: int32 [16], P(('grp', 'dev')), parts along dimension 0, may hold values from 0 to 7, as said below
- pair_count: int32 [8], P(('grp', 'dev')), parts along dimension 0, may hold values from 1 to 2, 6 in all
Outputs:
- layer_out: bfloat16 [1024, 3584], P(('grp', 'dev', 'tp')), parts along dimension 0
The draws below stay inside these ranges and needn't reach their ends.
There are 2 independent parts, one for each index of `grp`. The reference program is written for one: setup_inputs(seed, part) draws one part's arguments, and reference() takes and returns one part's arrays. A program takes and returns all parts, laid end to end along the dimension named above; an argument that names none is the same for every part. Nothing has to cross between parts.
Inputs may be any that keep to these rules, and one draw needn't show every extreme that they name: `pair_passage`: pair slot j belongs to owner floor(j / 2). Document owner k holds the ids k * 2 to (k + 1) * 2 - 1; the 2 slots of one owner name passages of 2 different document owners. Document owners with low k are named more often. Owner o's live pairs are its first pair_count[o] slots; the counts sum to 6.
All inputs are finite; a program needn't handle non-finite values. No bound on the sum of `pair_count` on one device may be relied on, other than what follows from the above.
Results may differ from the reference program's by a relative error of at most 0.012.
The reference program's roundings to bfloat16 on the way count: a program that leaves them out, or rounds other values in their place, can miss the bound.
Values may be sent and summed in bfloat16 or wider, within the bound.
A program may use at most 128 MiB of HBM per device.

```python
import math
import jax
import jax.numpy as jnp
import numpy as np
from jax import lax

D = 3584
H = 16
KVH = 8
HD = 256
PLEN = 512
QLEN = 64
P_DEV = 2
PAIR_DEV = 2
OWNERS = 4
PASSAGES = 8
PAIRS = 8
N_TP = 4


def planted_axes(key):
    direction_key, pattern_key = jax.random.split(key)
    direction = jax.random.rademacher(direction_key, (D,), dtype=jnp.float32) * D ** (-0.5)
    signs = jax.random.rademacher(pattern_key, (HD,), dtype=jnp.float32)
    half_width = HD // 2
    lane = jnp.arange(HD) % half_width
    pattern = jnp.where(lane >= half_width - 4, signs, 0.0) * 8.0 ** (-0.5)
    return (direction, pattern)


def drawn_weight(key, direction, pattern, heads, low, high):
    base_key, power_key = jax.random.split(key)
    base = jax.random.normal(base_key, (D, heads * HD)) * D ** (-0.5)
    power = jnp.exp(jax.random.uniform(power_key, (heads,), minval=jnp.log(low), maxval=jnp.log(high)))
    strength = jnp.sqrt(power) * HD ** 0.25
    planted = direction[:, None, None] * strength[None, :, None] * pattern[None, None, :]
    return jnp.clip(base + planted.reshape(D, heads * HD), -2.0, 2.0)


def draw_w_query(key, part):
    direction, pattern = planted_axes(key)
    key = jax.random.fold_in(key, 11)
    return drawn_weight(key, direction, pattern, H, 1.0, 40.0).astype(jnp.bfloat16)


def draw_w_key(key, part):
    direction, pattern = planted_axes(key)
    key = jax.random.fold_in(key, 13)
    return drawn_weight(key, direction, pattern, KVH, 1.0, 40.0).astype(jnp.bfloat16)


def draw_pair_passage(key, part):
    key = jax.random.fold_in(key, 7)
    owners = PAIRS // PAIR_DEV
    senders = PASSAGES // P_DEV
    noise_key, within_key = jax.random.split(key)
    noise = jax.random.randint(noise_key, (owners, senders), 0, 2 * senders)
    ranks = jnp.arange(senders, dtype=jnp.int32)
    value = noise - ranks[None, :] + senders
    forced = jnp.zeros((owners, senders), jnp.int32).at[0, 0].set(4 * senders).at[0, senders - 1].set(4 * senders)
    score = (value + forced) * senders + (senders - 1 - ranks)[None, :]
    top_scores, sender = lax.top_k(score, PAIR_DEV)
    within = jax.random.randint(within_key, (owners, senders), 0, P_DEV)
    within = within.at[0, senders - 1].set(P_DEV - 1).at[0, 0].set(0)
    chosen = jnp.take_along_axis(within, sender, axis=1)
    return (sender * P_DEV + chosen).reshape(PAIRS).astype(jnp.int32)


def block_levels(rng, dims, shards, least, top_value):
    level, own = 1.0, jax.random.fold_in(rng, 6)
    for position, parts in shards:
        steps = jnp.exp(jax.random.uniform(jax.random.fold_in(own, position), (parts,), jnp.float32, least / len(shards), top_value / len(shards)))
        level = level * jnp.repeat(steps, dims[position] // parts).reshape([-1 if axis == position else 1 for axis in range(len(dims))])
    return level


def split_up(count, total, reach, lean):
    portions = [(1 << 20) // math.isqrt(rank ** lean) + 1 for rank in range(2, count + 1)]
    surplus, counts = total - reach - (count - 1), [1] * (count - 1)
    while surplus > 0:
        candidates = [i for i in range(count - 1) if counts[i] < reach]
        pool, remaining = sum([portions[i] for i in candidates]), surplus
        for i in candidates:
            addition = min(reach - counts[i], max(1, remaining * portions[i] // pool), surplus)
            counts[i] = counts[i] + addition
            surplus = surplus - addition
    return np.array([reach] + counts)


def ragged(key, amount, total, reach, slope):
    if amount == 2:
        one = jax.random.randint(key, (), max(1, total - reach), min(reach, total - 1) + 1)
        return jnp.stack([one, total - one])
    tallies = jnp.asarray(split_up(amount, total, reach, slope), jnp.int32)
    pairs = (amount - 1) // 2
    source_of, sink = tallies[1:1 + 2 * pairs:2], tallies[2:2 + 2 * pairs:2]
    room = jnp.minimum(source_of - 1, reach - sink)
    passed = jax.random.randint(jax.random.fold_in(key, 1), (pairs,), 0, 1 << 20) % (room + 1)
    tallies = tallies.at[1:1 + 2 * pairs:2].set(source_of - passed).at[2:2 + 2 * pairs:2].set(sink + passed)
    return tallies[jax.random.permutation(jax.random.fold_in(key, 2), amount)]


def gaussian(own_key, dims, deviation, most, cuts=(), kind=jnp.bfloat16):
    values = jax.random.normal(own_key, dims, jnp.float32) * deviation
    if len(cuts) > 0:
        values = block_levels(own_key, dims, cuts, -0.22, 0.18) * values
    return jnp.clip(values, min=-most, max=most).astype(kind)


def setup_inputs(seed: int = 0, part: int = 0) -> dict:
    seeds = jax.random.split(jax.random.key(seed), 11)
    part_splits = jax.random.split(jax.random.fold_in(seeds[10], part), 11)
    return {
        "passage_hidden": gaussian(part_splits[0], (PASSAGES * PLEN, D), 1.0, 6.0, ((0, 16),)),
        "query_hidden": gaussian(part_splits[1], (PAIRS * QLEN, D), 1.0, 6.0, ((0, 16),)),
        "gain_in": jnp.clip(1.0 + 0.1 * jax.random.normal(seeds[2], (D,), jnp.float32), 0.5, 1.5).astype(jnp.bfloat16),
        "gain_out": jnp.clip(1.0 + 0.1 * jax.random.normal(seeds[3], (D,), jnp.float32), 0.5, 1.5).astype(jnp.bfloat16),
        "w_query": draw_w_query(jax.random.fold_in(seeds[10], 71), part),
        "w_key": draw_w_key(jax.random.fold_in(seeds[10], 71), part),
        "w_value": gaussian(seeds[6], (D, KVH * HD), D ** -0.5, 0.09375, ((1, 4),)),
        "w_out": gaussian(seeds[7], (H * HD, D), (H * HD) ** -0.5, 0.09375, ((0, 4),)),
        "pair_passage": draw_pair_passage(jax.random.fold_in(jax.random.fold_in(seeds[10], part), 71), part),
        "pair_count": ragged(part_splits[9], OWNERS, OWNERS * PAIR_DEV * 3 // 4, PAIR_DEV, 0).astype(jnp.int32),
    }


epsilon = 1e-06
softcap_limit = 50.0

def settle(values):
    return lax.optimization_barrier(values.astype(jnp.bfloat16)).astype(jnp.float32)

def normalize(rows, gain):
    values = rows.astype(jnp.float32)
    inverse_rms = lax.rsqrt(lax.optimization_barrier(jnp.mean(values * values, axis=-1, keepdims=True)) + epsilon)
    return (values * inverse_rms * gain.astype(jnp.float32)).astype(jnp.bfloat16)

def rotate(values, positions):
    head_width = values.shape[-1]
    half_width = head_width // 2
    frequency = 10000.0 ** (-2.0 * jnp.arange(half_width, dtype=jnp.float32) / head_width)
    angles = positions.astype(jnp.float32)[:, None] * frequency[None, :]
    cosine = jnp.cos(angles)[:, None, :]
    sine = jnp.sin(angles)[:, None, :]
    lower_half = values[..., :half_width]
    upper_half = values[..., half_width:]
    return jnp.concatenate([lower_half * cosine - upper_half * sine, upper_half * cosine + lower_half * sine], axis=-1)

def attend(query_rows, keys_own, values_own, keys_far, values_far):
    query_rows = query_rows.astype(jnp.float32)
    far_scores = jnp.einsum('qkgd,pkd->kgqp', query_rows, keys_far.astype(jnp.float32))
    near_scores = jnp.einsum('qkgd,tkd->kgqt', query_rows, keys_own.astype(jnp.float32))
    suffix_len = query_rows.shape[0]
    causal = jnp.arange(suffix_len)[:, None] >= jnp.arange(suffix_len)[None, :]
    far_weight = jnp.exp(softcap_limit * jnp.tanh(far_scores / softcap_limit))
    near_weight = jnp.where(causal, jnp.exp(softcap_limit * jnp.tanh(near_scores / softcap_limit)), 0.0)
    denominator = lax.optimization_barrier(jnp.sum(far_weight, axis=-1, keepdims=True)) + lax.optimization_barrier(jnp.sum(near_weight, axis=-1, keepdims=True))
    far_prob = (far_weight / denominator).astype(jnp.bfloat16).astype(jnp.float32)
    near_prob = (near_weight / denominator).astype(jnp.bfloat16).astype(jnp.float32)
    combined = jnp.einsum('kgqp,pkd->qkgd', far_prob, values_far.astype(jnp.float32))
    combined = combined + jnp.einsum('kgqt,tkd->qkgd', near_prob, values_own.astype(jnp.float32))
    return combined.astype(jnp.bfloat16).reshape(suffix_len, -1)

def reference(passage_hidden, query_hidden, gain_in, gain_out, w_query, w_key, w_value, w_out, pair_passage, pair_count):
    groups = H // KVH
    passage_norm = normalize(passage_hidden, gain_in)
    passage_pos = jnp.arange(PASSAGES * PLEN) % PLEN
    raw_keys = jnp.dot(passage_norm, w_key, preferred_element_type=jnp.float32).reshape(-1, KVH, HD)
    far_keys = rotate(raw_keys, passage_pos).astype(jnp.bfloat16).reshape(PASSAGES, PLEN, KVH, HD)
    far_values = jnp.dot(passage_norm, w_value, preferred_element_type=jnp.float32).astype(jnp.bfloat16).reshape(PASSAGES, PLEN, KVH, HD)
    query_norm = normalize(query_hidden, gain_in)
    query_pos = PLEN + jnp.arange(PAIRS * QLEN) % QLEN
    raw_queries = jnp.dot(query_norm, w_query, preferred_element_type=jnp.float32).reshape(-1, H, HD)
    queries = (rotate(raw_queries, query_pos) * HD ** (-0.5)).astype(jnp.bfloat16).reshape(PAIRS, QLEN, KVH, groups, HD)
    raw_own = jnp.dot(query_norm, w_key, preferred_element_type=jnp.float32).reshape(-1, KVH, HD)
    own_keys = rotate(raw_own, query_pos).astype(jnp.bfloat16).reshape(PAIRS, QLEN, KVH, HD)
    own_values = jnp.dot(query_norm, w_value, preferred_element_type=jnp.float32).astype(jnp.bfloat16).reshape(PAIRS, QLEN, KVH, HD)

    def one_pair(members):
        query_rows, keys_own, values_own, passage_row = members
        return attend(query_rows, keys_own, values_own, far_keys[passage_row], far_values[passage_row])
    attended = lax.map(one_pair, (queries, own_keys, own_values, pair_passage)).reshape(PAIRS * QLEN, H * HD)
    group_width = H * HD // N_TP
    merged = jnp.zeros((PAIRS * QLEN, D), jnp.float32)
    for shard in range(N_TP):
        lower = shard * group_width
        term = jnp.dot(attended[:, lower:lower + group_width], w_out[lower:lower + group_width], preferred_element_type=jnp.float32)
        merged = merged + settle(term)
    inverse_rms = lax.rsqrt(lax.optimization_barrier(jnp.mean(merged * merged, axis=-1, keepdims=True)) + epsilon)
    branch = merged * inverse_rms * gain_out.astype(jnp.float32)
    slot_ids = jnp.arange(PAIRS * QLEN) // QLEN
    alive = slot_ids % PAIR_DEV < pair_count[slot_ids // PAIR_DEV]
    layer_out = jnp.where(alive[:, None], query_hidden.astype(jnp.float32) + branch, 0.0)
    return layer_out.astype(jnp.bfloat16)
```

```python
import functools

import jax
import jax.numpy as jnp
import numpy as np
from jax import lax
from jax.experimental import pallas as pl
from jax.experimental.pallas import tpu as pltpu
from jax.sharding import PartitionSpec as P

HD = 256
HALF = HD // 2
PLEN = 512
QLEN = 64
CHUNKS = 2
VMEM_LIMIT = 48 * 1024 * 1024

epsilon = 1e-06
softcap_limit = 50.0


def tables(first, count):
    frequency = (10000.0 ** (-2.0 * np.arange(HALF, dtype=np.float32) / HD)).astype(np.float32)
    positions = np.arange(first, first + count, dtype=np.float32)
    angles = (positions[:, None] * frequency[None, :]).astype(np.float32)
    return jnp.asarray(np.cos(angles)), jnp.asarray(np.sin(angles))


def normalize(rows, gain):
    values = rows.astype(jnp.float32)
    inverse_rms = lax.rsqrt(jnp.mean(values * values, axis=-1, keepdims=True) + epsilon)
    return (values * inverse_rms * gain.astype(jnp.float32)).astype(jnp.bfloat16)


def turned(raw, cosine, sine):
    low, high = raw[:, :HALF], raw[:, HALF:]
    return jnp.concatenate([low * cosine - high * sine, high * cosine + low * sine], axis=1)


def params(aliased=False):
    return pltpu.CompilerParams(vmem_limit_bytes=VMEM_LIMIT)


def passage_body(heads_kv, aliased, place, rows_ref, wk_ref, wv_ref, cos_ref, sin_ref, *rest):
    out_ref = rest[-1]
    step = pl.program_id(0)

    @pl.when(step < heads_kv)
    def _():
        raw = jnp.dot(rows_ref[...], wk_ref[...], preferred_element_type=jnp.float32)
        out_ref[...] = turned(raw, cos_ref[...], sin_ref[...]).astype(jnp.bfloat16)

    @pl.when(step >= heads_kv)
    def _():
        raw = jnp.dot(rows_ref[...], wv_ref[...], preferred_element_type=jnp.float32)
        out_ref[...] = raw.astype(jnp.bfloat16)


def passage_project(block, place, total_rows, w_key, w_value, cosine, sine, held):
    count, width = block.shape
    heads_kv = w_key.shape[1] // HD
    per_passage = PLEN // count
    in_specs = [
        pl.BlockSpec((count, width), lambda j, place: (0, 0)),
        pl.BlockSpec((width, HD), lambda j, place: (0, jnp.minimum(j, heads_kv - 1))),
        pl.BlockSpec((width, HD), lambda j, place: (0, jnp.maximum(j - heads_kv, 0))),
        pl.BlockSpec((count, HALF), lambda j, place: (lax.rem(place[0], per_passage), 0)),
        pl.BlockSpec((count, HALF), lambda j, place: (lax.rem(place[0], per_passage), 0)),
    ]
    operands = [block, w_key, w_value, cosine, sine]
    aliases = {}
    if held is not None:
        in_specs.append(pl.BlockSpec(memory_space=pl.ANY))
        operands.append(held)
        aliases = {6: 0}
    return pl.pallas_call(
        functools.partial(passage_body, heads_kv, held is not None),
        grid_spec=pltpu.PrefetchScalarGridSpec(
            num_scalar_prefetch=1,
            grid=(2 * heads_kv,),
            in_specs=in_specs,
            out_specs=pl.BlockSpec((count, HD), lambda j, place: (place[0], j)),
        ),
        out_shape=jax.ShapeDtypeStruct((total_rows, 2 * heads_kv * HD), jnp.bfloat16),
        input_output_aliases=aliases,
        compiler_params=params(),
        cost_estimate=pl.CostEstimate(
            flops=4 * count * width * heads_kv * HD,
            bytes_accessed=4 * width * heads_kv * HD + 2 * count * width,
            transcendentals=0,
        ),
    )(place.reshape(1).astype(jnp.int32), *operands)


def query_body(n_blocks, n_out, heads_q, heads_kv, order, slot, *refs):
    blocks = refs[:n_blocks]
    gain_ref, wq_ref, wk_ref, wv_ref, cos_ref, sin_ref, out_ref, normed, held = refs[n_blocks:]
    step = pl.program_id(0)
    size = blocks[0].shape[0]

    @pl.when(step == 0)
    def _():
        for i in range(n_blocks):
            start = pl.multiple_of(order[i] * size, size)
            normed[pl.ds(start, size), :] = normalize(blocks[i][...], gain_ref[...])

    def store():
        for i in range(n_out):
            start = pl.multiple_of(slot[i] * QLEN, QLEN)
            out_ref[i] = held[pl.ds(start, QLEN), :].astype(jnp.bfloat16)

    @pl.when(step < heads_q)
    def _():
        raw = jnp.dot(normed[...], wq_ref[...], preferred_element_type=jnp.float32)
        held[...] = turned(raw, cos_ref[...], sin_ref[...]) * HD ** (-0.5)
        store()

    @pl.when((step >= heads_q) & (step < heads_q + heads_kv))
    def _():
        raw = jnp.dot(normed[...], wk_ref[...], preferred_element_type=jnp.float32)
        held[...] = turned(raw, cos_ref[...], sin_ref[...])
        store()

    @pl.when(step >= heads_q + heads_kv)
    def _():
        held[...] = jnp.dot(normed[...], wv_ref[...], preferred_element_type=jnp.float32)
        store()


def query_project(blocks, order, slot, gain, w_query, w_key, w_value, pair_slots):
    size, width = blocks[0].shape
    rows = size * len(blocks)
    heads_q, heads_kv = w_query.shape[1] // HD, w_key.shape[1] // HD
    n_out = slot.shape[0]
    cosine, sine = tables(PLEN, QLEN)
    cosine, sine = jnp.tile(cosine, (pair_slots, 1)), jnp.tile(sine, (pair_slots, 1))
    fixed = lambda j, order, slot: (0, 0)
    steps = heads_q + 2 * heads_kv
    return pl.pallas_call(
        functools.partial(query_body, len(blocks), n_out, heads_q, heads_kv),
        grid_spec=pltpu.PrefetchScalarGridSpec(
            num_scalar_prefetch=2,
            grid=(steps,),
            in_specs=[pl.BlockSpec((size, width), fixed) for _ in blocks]
            + [
                pl.BlockSpec((1, width), fixed),
                pl.BlockSpec((width, HD), lambda j, o, s: (0, jnp.minimum(j, heads_q - 1))),
                pl.BlockSpec(
                    (width, HD), lambda j, o, s: (0, jnp.clip(j - heads_q, 0, heads_kv - 1))
                ),
                pl.BlockSpec(
                    (width, HD), lambda j, o, s: (0, jnp.maximum(j - heads_q - heads_kv, 0))
                ),
                pl.BlockSpec((rows, HALF), fixed),
                pl.BlockSpec((rows, HALF), fixed),
            ],
            out_specs=pl.BlockSpec((n_out, QLEN, HD), lambda j, o, s: (0, 0, j)),
            scratch_shapes=[
                pltpu.VMEM((rows, width), jnp.bfloat16),
                pltpu.VMEM((rows, HD), jnp.float32),
            ],
        ),
        out_shape=jax.ShapeDtypeStruct((n_out, QLEN, steps * HD), jnp.bfloat16),
        compiler_params=params(),
        cost_estimate=pl.CostEstimate(
            flops=2 * rows * width * steps * HD,
            bytes_accessed=2 * width * steps * HD,
            transcendentals=0,
        ),
    )(order, slot, *blocks, gain.reshape(1, width), w_query, w_key, w_value, cosine, sine)


def capped_exp(scores):
    return jnp.exp(softcap_limit * jnp.tanh(scores / softcap_limit))


def attend_body(heads_q, heads_kv, within, pair_ref, far_ref, out_ref):
    groups = heads_q // heads_kv
    over = (((1,), (1,)), ((), ()))
    rows = lax.rem(lax.broadcasted_iota(jnp.int32, (groups * QLEN, QLEN), 0), QLEN)
    causal = rows >= lax.broadcasted_iota(jnp.int32, (groups * QLEN, QLEN), 1)
    for h in range(heads_kv):
        query = jnp.concatenate(
            [pair_ref[:, (h * groups + g) * HD : (h * groups + g + 1) * HD] for g in range(groups)],
            axis=0,
        )
        key_at, value_at = (heads_q + h) * HD, (heads_q + heads_kv + h) * HD
        keys_own = pair_ref[:, key_at : key_at + HD]
        values_own = pair_ref[:, value_at : value_at + HD]
        keys_far = far_ref[:, h * HD : (h + 1) * HD]
        values_far = far_ref[:, (heads_kv + h) * HD : (heads_kv + h + 1) * HD]
        far = capped_exp(
            lax.dot_general(query, keys_far, over, preferred_element_type=jnp.float32)
        )
        near = capped_exp(
            lax.dot_general(query, keys_own, over, preferred_element_type=jnp.float32)
        )
        near = jnp.where(causal, near, 0.0)
        total = jnp.sum(far, axis=1, keepdims=True) + jnp.sum(near, axis=1, keepdims=True)
        far = (far / total).astype(jnp.bfloat16)
        near = (near / total).astype(jnp.bfloat16)
        mixed = jnp.dot(far, values_far, preferred_element_type=jnp.float32)
        mixed = mixed + jnp.dot(near, values_own, preferred_element_type=jnp.float32)
        mixed = mixed.astype(jnp.bfloat16)
        for g in range(groups):
            at = (h * groups + g) * HD
            out_ref[:, at : at + HD] = mixed[g * QLEN : (g + 1) * QLEN]


def attend(pair, far, within, heads_q, heads_kv):
    return pl.pallas_call(
        functools.partial(attend_body, heads_q, heads_kv),
        grid_spec=pltpu.PrefetchScalarGridSpec(
            num_scalar_prefetch=1,
            grid=(1,),
            in_specs=[
                pl.BlockSpec(pair.shape, lambda j, w: (0, 0)),
                pl.BlockSpec((PLEN, far.shape[1]), lambda j, w: (w[0], 0)),
            ],
            out_specs=pl.BlockSpec((QLEN, heads_q * HD), lambda j, w: (0, 0)),
        ),
        out_shape=jax.ShapeDtypeStruct((QLEN, heads_q * HD), jnp.bfloat16),
        compiler_params=params(),
        cost_estimate=pl.CostEstimate(
            flops=4 * QLEN * (PLEN + QLEN) * heads_q * HD,
            bytes_accessed=2 * PLEN * far.shape[1],
            transcendentals=2 * QLEN * (PLEN + QLEN) * heads_q,
        ),
    )(within.reshape(1).astype(jnp.int32), pair, far)


def out_body(n_in, pair_slots, n_chips, where_ref, place, *refs):
    given = refs[:n_in]
    w_ref, keep_ref, give_ref, rows, held = refs[n_in:]
    size = keep_ref.shape[0] // n_chips

    @pl.when(pl.program_id(0) == 0)
    def _():
        for s in range(pair_slots):
            for i in range(n_in):

                @pl.when(where_ref[s] == i)
                def _():
                    rows[s * QLEN : (s + 1) * QLEN, :] = given[i][...]

    held[...] = jnp.dot(rows[...], w_ref[...], preferred_element_type=jnp.float32)
    for k in range(n_chips):
        chip = lax.rem(place[0] + k, n_chips)
        mine = pl.multiple_of((chip * 2 + place[1]) * size, size)
        twin = pl.multiple_of((chip * 2 + 1 - place[1]) * size, size)
        keep_ref[k * size : (k + 1) * size, :] = held[pl.ds(mine, size), :].astype(jnp.bfloat16)
        give_ref[k * size : (k + 1) * size, :] = held[pl.ds(twin, size), :].astype(jnp.bfloat16)


def out_project(given, sources, place, w_out, pair_slots, n_chips):
    depth, width = w_out.shape
    rows = pair_slots * QLEN
    tile = 512
    half = jax.ShapeDtypeStruct((rows // 2, width), jnp.bfloat16)
    return pl.pallas_call(
        functools.partial(out_body, len(given), pair_slots, n_chips),
        grid_spec=pltpu.PrefetchScalarGridSpec(
            num_scalar_prefetch=2,
            grid=(width // tile,),
            in_specs=[pl.BlockSpec((QLEN, depth), lambda j, a, b: (0, 0)) for _ in given]
            + [pl.BlockSpec((depth, tile), lambda j, a, b: (0, j))],
            out_specs=[pl.BlockSpec((rows // 2, tile), lambda j, a, b: (0, j))] * 2,
            scratch_shapes=[
                pltpu.VMEM((rows, depth), jnp.bfloat16),
                pltpu.VMEM((rows, tile), jnp.float32),
            ],
        ),
        out_shape=[half, half],
        compiler_params=params(),
        cost_estimate=pl.CostEstimate(
            flops=2 * rows * depth * width, bytes_accessed=2 * depth * width, transcendentals=0
        ),
    )(sources, place, *given, w_out)


def shards(
    passage_hidden,
    query_hidden,
    gain_in,
    gain_out,
    w_query,
    w_key,
    w_value,
    w_out,
    pair_passage,
    pair_count,
):
    n_tp, n_dev = lax.axis_size("tp"), lax.axis_size("dev")
    n_chips = n_tp // 2
    lane, owner = lax.axis_index("tp"), lax.axis_index("dev")
    chip, core = lane // 2, lane % 2
    heads_q, heads_kv = w_query.shape[1] // HD, w_key.shape[1] // HD
    pair_slots = pair_passage.shape[0]
    block_rows = passage_hidden.shape[0]
    total_rows = block_rows * n_tp
    per_owner = total_rows // PLEN

    def to_twin(values):
        return lax.ppermute(values, "tp", [(i, i ^ 1) for i in range(n_tp)])

    def from_chip(values, k):
        return lax.ppermute(values, "tp", [((i + 2 * k) % n_tp, i) for i in range(n_tp)])

    def to_owner(values, k):
        return lax.ppermute(values, "dev", [(i, (i + k) % n_dev) for i in range(n_dev)])

    def from_owner(values, k):
        return lax.ppermute(values, "dev", [((i + k) % n_dev, i) for i in range(n_dev)])

    query_blocks, query_order = [query_hidden, to_twin(query_hidden)], [lane, lane ^ 1]
    for k in range(1, n_chips):
        far = from_chip(query_hidden, k)
        base = (chip + k) % n_chips * 2
        query_blocks += [far, to_twin(far)]
        query_order += [base + core, base + 1 - core]
    shifts = [(owner + k) % n_dev for k in range(n_dev)]
    holder = pair_passage // per_owner
    slot = jnp.zeros((n_dev,), jnp.int32)
    for s in range(1, pair_slots):
        slot = jnp.where(holder[s] == jnp.stack(shifts), s, slot)
    named = [pair_passage] + [to_owner(pair_passage, k) for k in range(1, n_dev)]
    within = []
    for pairs in named:
        pick = pairs[0]
        for s in range(1, pair_slots):
            pick = jnp.where(pairs[s] // per_owner == owner, pairs[s], pick)
        within.append(pick % per_owner)

    normed = normalize(passage_hidden, gain_in)
    twin = to_twin(normed)
    unit = block_rows // CHUNKS
    arrivals = []
    for k in range(1, n_chips):
        for c in range(CHUNKS):
            far = from_chip(normed[c * unit : (c + 1) * unit], k)
            arrivals.append((k, c, far, to_twin(far)))

    projected = query_project(
        query_blocks,
        jnp.stack(query_order).astype(jnp.int32),
        slot,
        gain_in,
        w_query,
        w_key,
        w_value,
        pair_slots,
    )
    pairs = [projected[0]] + [to_owner(projected[k], k) for k in range(1, n_dev)]

    cosine, sine = tables(0, PLEN)
    project = functools.partial(
        passage_project, total_rows=total_rows, w_key=w_key, w_value=w_value, cosine=cosine, sine=sine
    )
    held = project(normed, lane, held=None)
    held = project(twin, lane ^ 1, held=held)
    for k, c, mine, other in arrivals:
        base = (chip + k) % n_chips * 2
        held = project(mine, (base + core) * CHUNKS + c, held=held)
        held = project(other, (base + 1 - core) * CHUNKS + c, held=held)

    mixed = [None] * n_dev
    for k in list(range(1, n_dev)) + [0]:
        result = attend(pairs[k], held, within[k], heads_q, heads_kv)
        mixed[k] = result if k == 0 else from_owner(result, k)

    sources = (holder - owner + n_dev) % n_dev
    keep, give = out_project(
        mixed,
        sources.astype(jnp.int32),
        jnp.stack([chip, core]).astype(jnp.int32),
        w_out,
        pair_slots,
        n_chips,
    )
    size = query_hidden.shape[0]
    summed = keep.astype(jnp.float32) + to_twin(give).astype(jnp.float32)
    merged = summed[:size]
    for k in range(1, n_chips):
        sent = summed[k * size : (k + 1) * size].astype(jnp.bfloat16)
        merged = merged + from_chip(sent, n_chips - k).astype(jnp.float32)
    inverse_rms = lax.rsqrt(jnp.mean(merged * merged, axis=-1, keepdims=True) + epsilon)
    branch = merged * inverse_rms * gain_out.astype(jnp.float32)
    row_ids = lane * size + jnp.arange(size)
    alive = row_ids // QLEN < pair_count[0]
    layer_out = jnp.where(alive[:, None], query_hidden.astype(jnp.float32) + branch, 0.0)
    return layer_out.astype(jnp.bfloat16)


def solution(mesh):
    placed = (
        P(("grp", "dev", "tp"), None),
        P(("grp", "dev", "tp"), None),
        P(),
        P(),
        P(None, "tp"),
        P(None, "tp"),
        P(None, "tp"),
        P("tp", None),
        P(("grp", "dev")),
        P(("grp", "dev")),
    )
    return jax.shard_map(
        shards, mesh=mesh, in_specs=placed, out_specs=P(("grp", "dev", "tp"), None), check_vma=False
    )
```

```python
import functools

import jax
import jax.numpy as jnp
import numpy as np
from jax import lax
from jax.experimental import pallas as pl
from jax.experimental.pallas import tpu as pltpu
from jax.sharding import PartitionSpec as P

HD = 256
HALF = HD // 2
PLEN = 512
QLEN = 64
CHUNKS = 4
TILE = 512
FLAG = 128
VMEM_LIMIT = 56 * 1024 * 1024
MESH = pl.DeviceIdType.MESH

epsilon = 1e-06
softcap_limit = 50.0


def tables(count):
    frequency = (10000.0 ** (-2.0 * np.arange(HALF, dtype=np.float32) / HD)).astype(np.float32)
    positions = np.arange(count, dtype=np.float32)
    angles = (positions[:, None] * frequency[None, :]).astype(np.float32)
    return jnp.asarray(np.stack([np.cos(angles), np.sin(angles)]))


def normalize(rows, gain):
    values = rows.astype(jnp.float32)
    inverse_rms = lax.rsqrt(jnp.mean(values * values, axis=-1, keepdims=True) + epsilon)
    return (values * inverse_rms * gain.astype(jnp.float32)).astype(jnp.bfloat16)


def turned(raw, cosine, sine):
    low, high = raw[:, :HALF], raw[:, HALF:]
    return jnp.concatenate([low * cosine - high * sine, high * cosine + low * sine], axis=1)


def capped_exp(scores):
    return jnp.exp(softcap_limit * jnp.tanh(scores / softcap_limit))


def columns(j, width):
    return pl.ds(pl.multiple_of(j * width, width), width)


def attend(pair_ref, held_ref, out_ref, heads_q, heads_kv, per_owner):
    groups = heads_q // heads_kv
    over = (((1,), (1,)), ((), ()))
    rows = lax.rem(lax.broadcasted_iota(jnp.int32, (groups * QLEN, QLEN), 0), QLEN)
    causal = rows >= lax.broadcasted_iota(jnp.int32, (groups * QLEN, QLEN), 1)
    flag_at = (heads_q + 2 * heads_kv) * HD
    flag = pair_ref[:, flag_at : flag_at + FLAG].astype(jnp.float32)[:, :1]
    flag = jnp.concatenate([flag] * groups, axis=0)
    for h in range(heads_kv):
        query = jnp.concatenate(
            [pair_ref[:, (h * groups + g) * HD : (h * groups + g + 1) * HD] for g in range(groups)],
            axis=0,
        )
        key_at, value_at = (heads_q + h) * HD, (heads_q + heads_kv + h) * HD
        keys_own = pair_ref[:, key_at : key_at + HD]
        values_own = pair_ref[:, value_at : value_at + HD]
        far = None
        for p in range(per_owner):
            keys = held_ref[p * PLEN : (p + 1) * PLEN, h * HD : (h + 1) * HD]
            scores = lax.dot_general(query, keys, over, preferred_element_type=jnp.float32)
            far = scores if p == 0 else jnp.where(flag == float(p), scores, far)
        far = capped_exp(far)
        near = capped_exp(
            lax.dot_general(query, keys_own, over, preferred_element_type=jnp.float32)
        )
        near = jnp.where(causal, near, 0.0)
        total = jnp.sum(far, axis=1, keepdims=True) + jnp.sum(near, axis=1, keepdims=True)
        far = far / total
        near = (near / total).astype(jnp.bfloat16)
        mixed = jnp.dot(near, values_own, preferred_element_type=jnp.float32)
        for p in range(per_owner):
            at = (heads_kv + h) * HD
            values = held_ref[p * PLEN : (p + 1) * PLEN, at : at + HD]
            weights = jnp.where(flag == float(p), far, 0.0).astype(jnp.bfloat16)
            mixed = mixed + jnp.dot(weights, values, preferred_element_type=jnp.float32)
        mixed = mixed.astype(jnp.bfloat16)
        for g in range(groups):
            at = (h * groups + g) * HD
            out_ref[:, at : at + HD] = mixed[g * QLEN : (g + 1) * QLEN]


def body(
    n_tp, n_dev,
    pairs_ref, count_ref, gain_in_ref, gain_out_ref, passage_ref, query_ref, table_ref,
    wq_ref, wk_ref, wv_ref, wo_ref, out_ref,
    raw, passage, held, gathered, suffix, turn, pack, received, mixed, returned, attended,
    wq, wk, wv, wo, work, product, keep, give, twin_in, sums, sums_in, merged,
    load_sem, raw_sem, query_send, query_recv, near_send, far_send, pass_send, rows_recv,
    pair_send, pair_recv, back_send, back_recv, give_send, give_recv, sum_send, sum_recv,
):
    n_chips = n_tp // 2
    lane, owner = lax.axis_index("tp"), lax.axis_index("dev")
    chip, core = lane // 2, lane % 2
    twin = chip * 2 + 1 - core
    heads_q, heads_kv = wq.shape[1] // HD, wk.shape[1] // HD
    block_rows, width = raw.shape
    unit = block_rows // CHUNKS
    size = query_ref.shape[0]
    per_owner = block_rows * n_tp // PLEN
    pair_slots = pairs_ref.shape[0]
    n_cols = width // TILE

    def peer(k):
        return lax.rem(chip + k, n_chips) * 2 + core

    def send(src, dst, send_sem, recv_sem, axis, target):
        copy = pltpu.make_async_remote_copy(
            src_ref=src, dst_ref=dst, send_sem=send_sem, recv_sem=recv_sem,
            device_id={axis: target}, device_id_type=MESH,
        )
        copy.start()

    def sent(ref, sem):
        pltpu.make_async_remote_copy(
            src_ref=ref, dst_ref=ref, send_sem=sem, recv_sem=sem,
            device_id={"tp": twin}, device_id_type=MESH,
        ).wait_send()

    def arrived(ref, sem):
        pltpu.make_async_remote_copy(
            src_ref=ref, dst_ref=ref, send_sem=sem, recv_sem=sem,
            device_id={"tp": twin}, device_id_type=MESH,
        ).wait_recv()

    def in_range(names, holder):
        return (names >= holder * per_owner) & (names < (holder + 1) * per_owner)

    for c in range(CHUNKS):
        at = pl.ds(c * unit, unit)
        pltpu.make_async_copy(passage_ref.at[at], raw.at[at], raw_sem.at[c]).start()
    loads = [
        pltpu.make_async_copy(query_ref, gathered.at[lane], load_sem.at[0]),
        pltpu.make_async_copy(table_ref, turn, load_sem.at[1]),
        pltpu.make_async_copy(wk_ref, wk, load_sem.at[2]),
        pltpu.make_async_copy(wv_ref, wv, load_sem.at[3]),
        pltpu.make_async_copy(wq_ref, wq, load_sem.at[4]),
        pltpu.make_async_copy(wo_ref, wo, load_sem.at[5]),
    ]
    for load in loads:
        load.start()

    barrier = pltpu.get_barrier_semaphore()
    pl.semaphore_signal(barrier, inc=1, device_id={"tp": twin}, device_id_type=MESH)
    for k in range(1, n_chips):
        pl.semaphore_signal(barrier, inc=1, device_id={"tp": peer(k)}, device_id_type=MESH)
    for k in range(1, n_dev):
        there = lax.rem(owner + k, n_dev)
        pl.semaphore_signal(barrier, inc=1, device_id={"dev": there}, device_id_type=MESH)
    pl.semaphore_wait(barrier, n_chips + n_dev - 1)

    for k in range(1, n_chips):
        send(query_ref, gathered.at[lane], query_send.at[k], query_recv.at[lane], "tp", peer(k))
    send(query_ref, gathered.at[lane], query_send.at[0], query_recv.at[lane], "tp", twin)

    def norm_chunk(c, carry):
        at = pl.ds(pl.multiple_of(c * unit, unit), unit)
        pltpu.make_async_copy(passage_ref.at[at], raw.at[at], raw_sem.at[c]).wait()
        passage[lane, at, :] = normalize(raw[at, :], gain_in_ref[...])
        mine = passage.at[lane, at]
        for k in range(1, n_chips):
            send(mine, mine, far_send.at[k - 1, c], rows_recv.at[lane, c], "tp", peer(k))
        send(mine, mine, near_send.at[c], rows_recv.at[lane, c], "tp", twin)
        return carry

    lax.fori_loop(0, CHUNKS, norm_chunk, 0)

    def project(block, first, rows):
        row = block * block_rows + first
        place = pl.multiple_of(row, rows)
        spot = pl.ds(pl.multiple_of(lax.rem(row, PLEN), rows), rows)

        def keys(j, carry):
            weights = wk[:, columns(j, HD)]
            product_ = jnp.dot(
                passage[block, pl.ds(first, rows), :], weights, preferred_element_type=jnp.float32
            )
            held[pl.ds(place, rows), columns(j, HD)] = turned(
                product_, turn[0, spot, :], turn[1, spot, :]
            ).astype(jnp.bfloat16)
            return carry

        def values(j, carry):
            weights = wv[:, columns(j, HD)]
            product_ = jnp.dot(
                passage[block, pl.ds(first, rows), :], weights, preferred_element_type=jnp.float32
            )
            held[pl.ds(place, rows), columns(heads_kv + j, HD)] = product_.astype(jnp.bfloat16)
            return carry

        lax.fori_loop(0, heads_kv, keys, 0)
        lax.fori_loop(0, heads_kv, values, 0)

    for load in loads[1:4]:
        load.wait()
    project(lane, 0, block_rows)

    for k in range(1, n_chips):
        arrived(gathered.at[peer(k)], query_recv.at[peer(k)])
        block = gathered.at[peer(k)]
        send(block, block, query_send.at[n_chips + k - 1], query_recv.at[peer(k)], "tp", twin)
    arrived(gathered.at[twin], query_recv.at[twin])
    for k in range(1, n_chips):
        other = lax.rem(chip + k, n_chips) * 2 + 1 - core
        arrived(gathered.at[other], query_recv.at[other])
    loads[0].wait()
    for i in range(n_tp):
        suffix[i * size : (i + 1) * size, :] = normalize(gathered[i], gain_in_ref[...])
    flag_at = (heads_q + 2 * heads_kv) * HD
    for k in range(n_dev):
        there = lax.rem(owner + k, n_dev)
        name = jnp.full((QLEN, FLAG), pairs_ref[0])
        for s in range(1, pair_slots):
            other = jnp.full((QLEN, FLAG), pairs_ref[s])
            name = jnp.where(in_range(other, there), other, name)
        flag = jnp.zeros((QLEN, FLAG), jnp.float32)
        for p in range(1, per_owner):
            for o in range(n_dev):
                flag = jnp.where(name == o * per_owner + p, float(p), flag)
        pack[k, :, flag_at : flag_at + FLAG] = flag.astype(jnp.bfloat16)
    loads[4].wait()

    def store(j):
        for k in range(n_dev):
            there = lax.rem(owner + k, n_dev)
            rows = work[:QLEN, :]
            for s in range(1, pair_slots):
                hit = in_range(jnp.full((QLEN, HD), pairs_ref[s]), there)
                rows = jnp.where(hit, work[s * QLEN : (s + 1) * QLEN, :], rows)
            pack[k, :, columns(j, HD)] = rows.astype(jnp.bfloat16)

    def spun(values):
        cosine = jnp.concatenate([turn[0, PLEN : PLEN + QLEN, :]] * pair_slots, axis=0)
        sine = jnp.concatenate([turn[1, PLEN : PLEN + QLEN, :]] * pair_slots, axis=0)
        return turned(values, cosine, sine)

    def suffix_queries(j, carry):
        raw_ = jnp.dot(suffix[...], wq[:, columns(j, HD)], preferred_element_type=jnp.float32)
        work[...] = spun(raw_) * HD ** (-0.5)
        store(j)
        return carry

    def suffix_keys(j, carry):
        raw_ = jnp.dot(suffix[...], wk[:, columns(j, HD)], preferred_element_type=jnp.float32)
        work[...] = spun(raw_)
        store(heads_q + j)
        return carry

    def suffix_values(j, carry):
        work[...] = jnp.dot(suffix[...], wv[:, columns(j, HD)], preferred_element_type=jnp.float32)
        store(heads_q + heads_kv + j)
        return carry

    lax.fori_loop(0, heads_q, suffix_queries, 0)
    lax.fori_loop(0, heads_kv, suffix_keys, 0)
    lax.fori_loop(0, heads_kv, suffix_values, 0)
    for k in range(1, n_dev):
        there = lax.rem(owner + k, n_dev)
        send(pack.at[k], received.at[k - 1], pair_send.at[k - 1], pair_recv.at[k - 1], "dev", there)

    for c in range(CHUNKS):
        at = pl.ds(c * unit, unit)
        arrived(passage.at[twin, at], rows_recv.at[twin, c])
    project(twin, 0, block_rows)
    for k in range(1, n_chips):
        here = peer(k)
        other = lax.rem(chip + k, n_chips) * 2 + 1 - core

        def step(i, carry):
            for half in range(2):
                c = i * 2 + half
                rows = passage.at[here, pl.ds(pl.multiple_of(c * unit, unit), unit)]
                arrived(rows, rows_recv.at[here, c])
                send(rows, rows, pass_send.at[k - 1, c], rows_recv.at[here, c], "tp", twin)
            first = pl.multiple_of(i * 2 * unit, 2 * unit)
            project(here, first, 2 * unit)
            for half in range(2):
                c = i * 2 + half
                rows = passage.at[other, pl.ds(pl.multiple_of(c * unit, unit), unit)]
                arrived(rows, rows_recv.at[other, c])
            project(other, first, 2 * unit)
            return carry

        lax.fori_loop(0, CHUNKS // 2, step, 0)

    def pair_step(i, carry):
        arrived(received.at[i], pair_recv.at[i])
        attend(received.at[i], held, mixed.at[i], heads_q, heads_kv, per_owner)
        back = lax.rem(owner + n_dev - 1 - i, n_dev)
        send(mixed.at[i], returned.at[i + 1], back_send.at[i], back_recv.at[i], "dev", back)
        return carry

    lax.fori_loop(0, n_dev - 1, pair_step, 0)
    attend(pack.at[0], held, returned.at[0], heads_q, heads_kv, per_owner)
    loads[5].wait()
    for i in range(n_dev - 1):
        arrived(returned.at[i + 1], back_recv.at[i])
    for s in range(pair_slots):
        name = jnp.full(returned.shape[1:], pairs_ref[s])
        rows = returned[0].astype(jnp.float32)
        for k in range(1, n_dev):
            there = lax.rem(owner + k, n_dev)
            rows = jnp.where(in_range(name, there), returned[k].astype(jnp.float32), rows)
        attended[s * QLEN : (s + 1) * QLEN, :] = rows.astype(jnp.bfloat16)

    def pass_on(j):
        arrived(twin_in.at[j], give_recv.at[j])
        summed = keep[j].astype(jnp.float32) + twin_in[j].astype(jnp.float32)
        merged[j] = summed[:size]
        for k in range(1, n_chips):
            sums[k - 1, j] = summed[k * size : (k + 1) * size].astype(jnp.bfloat16)
            send(
                sums.at[k - 1, j], sums_in.at[k - 1, j],
                sum_send.at[k - 1, j], sum_recv.at[k - 1, j], "tp", peer(k),
            )

    def out_step(j, carry):
        product[...] = jnp.dot(
            attended[...], wo[:, columns(j, TILE)], preferred_element_type=jnp.float32
        )
        for k in range(n_chips):
            base = lax.rem(chip + k, n_chips) * 2
            mine = pl.multiple_of((base + core) * size, size)
            theirs = pl.multiple_of((base + 1 - core) * size, size)
            at = pl.ds(k * size, size)
            keep[j, at, :] = product[pl.ds(mine, size), :].astype(jnp.bfloat16)
            give[j, at, :] = product[pl.ds(theirs, size), :].astype(jnp.bfloat16)
        send(give.at[j], twin_in.at[j], give_send.at[j], give_recv.at[j], "tp", twin)

        @pl.when(j > 0)
        def _():
            pass_on(j - 1)

        return carry

    lax.fori_loop(0, n_cols, out_step, 0)
    pass_on(n_cols - 1)
    squares = jnp.zeros((size, 1), jnp.float32)
    for j in range(n_cols):
        total = merged[j]
        for k in range(1, n_chips):
            arrived(sums_in.at[k - 1, j], sum_recv.at[k - 1, j])
            total = total + sums_in[k - 1, j].astype(jnp.float32)
        merged[j] = total
        squares = squares + jnp.sum(total * total, axis=1, keepdims=True)
    scale = lax.rsqrt(squares / width + epsilon)
    row_ids = lane * size + lax.broadcasted_iota(jnp.int32, (size, TILE), 0)
    alive = row_ids < count_ref[0] * QLEN
    for j in range(n_cols):
        at = slice(j * TILE, (j + 1) * TILE)
        branch = merged[j] * scale * gain_out_ref[:, at].astype(jnp.float32)
        whole = gathered[lane, :, at].astype(jnp.float32) + branch
        out_ref[:, at] = jnp.where(alive, whole, 0.0).astype(jnp.bfloat16)

    for k in range(2 * n_chips - 1):
        sent(gathered.at[0], query_send.at[k])
    for c in range(CHUNKS):
        rows = passage.at[0, pl.ds(0, unit)]
        sent(rows, near_send.at[c])
        for k in range(n_chips - 1):
            sent(rows, far_send.at[k, c])
            sent(rows, pass_send.at[k, c])
    for i in range(n_dev - 1):
        sent(received.at[i], pair_send.at[i])
        sent(mixed.at[i], back_send.at[i])
    for j in range(n_cols):
        sent(give.at[j], give_send.at[j])
        for k in range(n_chips - 1):
            sent(sums.at[k, j], sum_send.at[k, j])


def shards(
    passage_hidden,
    query_hidden,
    gain_in,
    gain_out,
    w_query,
    w_key,
    w_value,
    w_out,
    pair_passage,
    pair_count,
):
    n_tp, n_dev = lax.axis_size("tp"), lax.axis_size("dev")
    n_chips = n_tp // 2
    pair_slots = pair_passage.shape[0]
    block_rows, width = passage_hidden.shape
    size = query_hidden.shape[0]
    rows = pair_slots * QLEN
    wide_q, wide_kv = w_query.shape[1], w_key.shape[1]
    pack_width = wide_q + 2 * wide_kv + FLAG
    n_cols = width // TILE
    half = rows // 2
    bf, f32, dma = jnp.bfloat16, jnp.float32, pltpu.SemaphoreType.DMA
    smem = pl.BlockSpec(memory_space=pltpu.SMEM)
    vmem = pl.BlockSpec(memory_space=pltpu.VMEM)
    hbm = pl.BlockSpec(memory_space=pl.ANY)
    far = n_chips - 1
    return pl.pallas_call(
        functools.partial(body, n_tp, n_dev),
        out_shape=jax.ShapeDtypeStruct((size, width), bf),
        in_specs=[smem, smem, vmem, vmem] + [hbm] * 7,
        out_specs=vmem,
        scratch_shapes=[
            pltpu.VMEM((block_rows, width), bf),
            pltpu.VMEM((n_tp, block_rows, width), bf),
            pltpu.VMEM((n_tp * block_rows, 2 * wide_kv), bf),
            pltpu.VMEM((n_tp, size, width), bf),
            pltpu.VMEM((rows, width), bf),
            pltpu.VMEM((2, PLEN + QLEN, HALF), f32),
            pltpu.VMEM((n_dev, QLEN, pack_width), bf),
            pltpu.VMEM((n_dev - 1, QLEN, pack_width), bf),
            pltpu.VMEM((n_dev - 1, QLEN, wide_q), bf),
            pltpu.VMEM((n_dev, QLEN, wide_q), bf),
            pltpu.VMEM((rows, wide_q), bf),
            pltpu.VMEM(w_query.shape, bf),
            pltpu.VMEM(w_key.shape, bf),
            pltpu.VMEM(w_value.shape, bf),
            pltpu.VMEM(w_out.shape, bf),
            pltpu.VMEM((rows, HD), f32),
            pltpu.VMEM((rows, TILE), f32),
            pltpu.VMEM((n_cols, half, TILE), bf),
            pltpu.VMEM((n_cols, half, TILE), bf),
            pltpu.VMEM((n_cols, half, TILE), bf),
            pltpu.VMEM((far, n_cols, size, TILE), bf),
            pltpu.VMEM((far, n_cols, size, TILE), bf),
            pltpu.VMEM((n_cols, size, TILE), f32),
            dma((6,)),
            dma((CHUNKS,)),
            dma((2 * n_chips - 1,)),
            dma((n_tp,)),
            dma((CHUNKS,)),
            dma((far, CHUNKS)),
            dma((far, CHUNKS)),
            dma((n_tp, CHUNKS)),
            dma((n_dev - 1,)),
            dma((n_dev - 1,)),
            dma((n_dev - 1,)),
            dma((n_dev - 1,)),
            dma((n_cols,)),
            dma((n_cols,)),
            dma((far, n_cols)),
            dma((far, n_cols)),
        ],
        compiler_params=pltpu.CompilerParams(
            collective_id=0, has_side_effects=True, vmem_limit_bytes=VMEM_LIMIT
        ),
    )(
        pair_passage,
        pair_count,
        gain_in.reshape(1, width),
        gain_out.reshape(1, width),
        passage_hidden,
        query_hidden,
        tables(PLEN + QLEN),
        w_query,
        w_key,
        w_value,
        w_out,
    )


def solution(mesh):
    placed = (
        P(("grp", "dev", "tp"), None),
        P(("grp", "dev", "tp"), None),
        P(),
        P(),
        P(None, "tp"),
        P(None, "tp"),
        P(None, "tp"),
        P("tp", None),
        P(("grp", "dev")),
        P(("grp", "dev")),
    )
    return jax.shard_map(
        shards, mesh=mesh, in_specs=placed, out_specs=P(("grp", "dev", "tp"), None), check_vma=False
    )
```

```python
import functools

import jax
import jax.numpy as jnp
import numpy as np
from jax import lax
from jax.experimental import pallas as pl
from jax.experimental.pallas import tpu as pltpu
from jax.sharding import PartitionSpec as P

HD = 256
HALF = HD // 2
PLEN = 512
QLEN = 64
CHUNKS = 4
TILE = 512
FLAG = 128
VMEM_LIMIT = 56 * 1024 * 1024
MESH = pl.DeviceIdType.MESH

epsilon = 1e-06
softcap_limit = 50.0


def tables(count):
    frequency = (10000.0 ** (-2.0 * np.arange(HALF, dtype=np.float32) / HD)).astype(np.float32)
    positions = np.arange(count, dtype=np.float32)
    angles = (positions[:, None] * frequency[None, :]).astype(np.float32)
    return jnp.asarray(np.stack([np.cos(angles), np.sin(angles)]))


def normalize(rows, gain):
    values = rows.astype(jnp.float32)
    inverse_rms = lax.rsqrt(jnp.mean(values * values, axis=-1, keepdims=True) + epsilon)
    return (values * inverse_rms * gain).astype(jnp.bfloat16)


def turned(raw, cosine, sine):
    low, high = raw[:, :HALF], raw[:, HALF:]
    return jnp.concatenate([low * cosine - high * sine, high * cosine + low * sine], axis=1)


def capped_exp(scores):
    return jnp.exp(softcap_limit * jnp.tanh(scores * (1.0 / softcap_limit)))


def columns(j, width):
    return pl.ds(pl.multiple_of(j * width, width), width)


def attend(pair_ref, held_ref, out_ref, heads_q, heads_kv, passages, other_ref=None):
    groups = heads_q // heads_kv
    over = (((1,), (1,)), ((), ()))
    rows = lax.rem(lax.broadcasted_iota(jnp.int32, (groups * QLEN, QLEN), 0), QLEN)
    causal = rows >= lax.broadcasted_iota(jnp.int32, (groups * QLEN, QLEN), 1)
    flag_at = (heads_q + 2 * heads_kv) * HD
    flag = pair_ref[:, flag_at : flag_at + FLAG].astype(jnp.float32)[:, :1]
    flag = jnp.concatenate([flag] * groups, axis=0)
    for h in range(heads_kv):
        query = jnp.concatenate(
            [pair_ref[:, (h * groups + g) * HD : (h * groups + g + 1) * HD] for g in range(groups)],
            axis=0,
        )
        key_at, value_at = (heads_q + h) * HD, (heads_q + heads_kv + h) * HD
        keys_own = pair_ref[:, key_at : key_at + HD]
        values_own = pair_ref[:, value_at : value_at + HD]
        far = None
        for i, p in enumerate(passages):
            keys = held_ref[columns(p, PLEN), h * HD : (h + 1) * HD]
            scores = lax.dot_general(query, keys, over, preferred_element_type=jnp.float32)
            far = scores if i == 0 else jnp.where(flag == jnp.float32(p), scores, far)
        far = capped_exp(far)
        near = capped_exp(
            lax.dot_general(query, keys_own, over, preferred_element_type=jnp.float32)
        )
        near = jnp.where(causal, near, 0.0)
        total = jnp.sum(far, axis=1, keepdims=True) + jnp.sum(near, axis=1, keepdims=True)
        inverse = 1.0 / total
        far = far * inverse
        near = (near * inverse).astype(jnp.bfloat16)
        mixed = jnp.dot(near, values_own, preferred_element_type=jnp.float32)
        for p in passages:
            at = (heads_kv + h) * HD
            values = held_ref[columns(p, PLEN), at : at + HD]
            weights = far if len(passages) == 1 else jnp.where(flag == jnp.float32(p), far, 0.0)
            weights = weights.astype(jnp.bfloat16)
            mixed = mixed + jnp.dot(weights, values, preferred_element_type=jnp.float32)
        for g in range(groups):
            at = (h * groups + g) * HD
            part = mixed[g * QLEN : (g + 1) * QLEN]
            if other_ref is not None:
                chosen = flag[:QLEN] == passages[0].astype(jnp.float32)
                part = jnp.where(chosen, part, other_ref[:, at : at + HD].astype(jnp.float32))
            out_ref[:, at : at + HD] = part.astype(jnp.bfloat16)


def body(
    n_tp, n_dev,
    pairs_ref, count_ref, gain_in_ref, gain_out_ref, passage_ref, query_ref, table_ref,
    wq_ref, wk_ref, wv_ref, wo_ref, out_ref,
    raw, passage, held, gathered, suffix, turn, pack, received, mixed, early, returned, attended,
    wq, wk, wv, wo, work, product, keep, give, twin_in, sums, sums_in, merged,
    load_sem, raw_sem, query_send, query_recv, near_send, far_send, pass_send, rows_recv,
    pair_send, pair_recv, back_send, back_recv, give_send, give_recv, sum_send, sum_recv,
):
    n_chips = n_tp // 2
    lane, owner = lax.axis_index("tp"), lax.axis_index("dev")
    chip, core = lane // 2, lane % 2
    twin = chip * 2 + 1 - core
    heads_q, heads_kv = wq.shape[1] // HD, wk.shape[1] // HD
    block_rows, width = raw.shape
    unit = block_rows // CHUNKS
    size = query_ref.shape[0]
    per_owner = block_rows * n_tp // PLEN
    pair_slots = pairs_ref.shape[0]
    n_cols = width // TILE
    halves = n_chips == 2 and per_owner == 2

    def peer(k):
        return lax.rem(chip + k, n_chips) * 2 + core

    def send(src, dst, send_sem, recv_sem, axis, target):
        copy = pltpu.make_async_remote_copy(
            src_ref=src, dst_ref=dst, send_sem=send_sem, recv_sem=recv_sem,
            device_id={axis: target}, device_id_type=MESH,
        )
        copy.start()

    def sent(ref, sem):
        pltpu.make_async_remote_copy(
            src_ref=ref, dst_ref=ref, send_sem=sem, recv_sem=sem,
            device_id={"tp": twin}, device_id_type=MESH,
        ).wait_send()

    def arrived(ref, sem):
        pltpu.make_async_remote_copy(
            src_ref=ref, dst_ref=ref, send_sem=sem, recv_sem=sem,
            device_id={"tp": twin}, device_id_type=MESH,
        ).wait_recv()

    def in_range(names, holder):
        return (names >= holder * per_owner) & (names < (holder + 1) * per_owner)

    for c in range(CHUNKS):
        at = pl.ds(c * unit, unit)
        pltpu.make_async_copy(passage_ref.at[at], raw.at[at], raw_sem.at[c]).start()
    loads = [
        pltpu.make_async_copy(query_ref, gathered.at[lane], load_sem.at[0]),
        pltpu.make_async_copy(table_ref, turn, load_sem.at[1]),
        pltpu.make_async_copy(wk_ref, wk, load_sem.at[2]),
        pltpu.make_async_copy(wv_ref, wv, load_sem.at[3]),
        pltpu.make_async_copy(wq_ref, wq, load_sem.at[4]),
        pltpu.make_async_copy(wo_ref, wo, load_sem.at[5]),
    ]
    for load in loads:
        load.start()

    barrier = pltpu.get_barrier_semaphore()
    pl.semaphore_signal(barrier, inc=1, device_id={"tp": twin}, device_id_type=MESH)
    for k in range(1, n_chips):
        pl.semaphore_signal(barrier, inc=1, device_id={"tp": peer(k)}, device_id_type=MESH)
    for k in range(1, n_dev):
        there = lax.rem(owner + k, n_dev)
        pl.semaphore_signal(barrier, inc=1, device_id={"dev": there}, device_id_type=MESH)
    pl.semaphore_wait(barrier, n_chips + n_dev - 1)

    for k in range(1, n_chips):
        send(query_ref, gathered.at[lane], query_send.at[k], query_recv.at[lane], "tp", peer(k))
    send(query_ref, gathered.at[lane], query_send.at[0], query_recv.at[lane], "tp", twin)

    def norm_chunk(c, carry):
        at = pl.ds(pl.multiple_of(c * unit, unit), unit)
        pltpu.make_async_copy(passage_ref.at[at], raw.at[at], raw_sem.at[c]).wait()
        passage[lane, at, :] = normalize(raw[at, :], gain_in_ref[...].astype(jnp.float32).reshape(1, width))
        mine = passage.at[lane, at]
        for k in range(1, n_chips):
            send(mine, mine, far_send.at[k - 1, c], rows_recv.at[lane, c], "tp", peer(k))
        send(mine, mine, near_send.at[c], rows_recv.at[lane, c], "tp", twin)
        return carry

    lax.fori_loop(0, CHUNKS, norm_chunk, 0)

    def project(block, first, rows):
        row = block * block_rows + first
        place = pl.multiple_of(row, rows)
        spot = pl.ds(pl.multiple_of(lax.rem(row, PLEN), rows), rows)

        def keys(j, carry):
            weights = wk[:, columns(j, HD)]
            product_ = jnp.dot(
                passage[block, pl.ds(first, rows), :], weights, preferred_element_type=jnp.float32
            )
            held[pl.ds(place, rows), columns(j, HD)] = turned(
                product_, turn[0, spot, :], turn[1, spot, :]
            ).astype(jnp.bfloat16)
            return carry

        def values(j, carry):
            weights = wv[:, columns(j, HD)]
            product_ = jnp.dot(
                passage[block, pl.ds(first, rows), :], weights, preferred_element_type=jnp.float32
            )
            held[pl.ds(place, rows), columns(heads_kv + j, HD)] = product_.astype(jnp.bfloat16)
            return carry

        lax.fori_loop(0, heads_kv, keys, 0)
        lax.fori_loop(0, heads_kv, values, 0)

    for load in loads[1:4]:
        load.wait()
    project(lane, 0, block_rows)

    for k in range(1, n_chips):
        arrived(gathered.at[peer(k)], query_recv.at[peer(k)])
        block = gathered.at[peer(k)]
        send(block, block, query_send.at[n_chips + k - 1], query_recv.at[peer(k)], "tp", twin)
    arrived(gathered.at[twin], query_recv.at[twin])
    for k in range(1, n_chips):
        other = lax.rem(chip + k, n_chips) * 2 + 1 - core
        arrived(gathered.at[other], query_recv.at[other])
    loads[0].wait()
    for i in range(n_tp):
        suffix[i * size : (i + 1) * size, :] = normalize(gathered[i], gain_in_ref[...].astype(jnp.float32).reshape(1, width))
    flag_at = (heads_q + 2 * heads_kv) * HD
    for k in range(n_dev):
        there = lax.rem(owner + k, n_dev)
        name = jnp.full((QLEN, FLAG), pairs_ref[0])
        for s in range(1, pair_slots):
            other = jnp.full((QLEN, FLAG), pairs_ref[s])
            name = jnp.where(in_range(other, there), other, name)
        flag = jnp.zeros((QLEN, FLAG), jnp.float32)
        for p in range(1, per_owner):
            for o in range(n_dev):
                flag = jnp.where(name == o * per_owner + p, float(p), flag)
        pack[k, :, flag_at : flag_at + FLAG] = flag.astype(jnp.bfloat16)
    loads[4].wait()

    def store(j):
        for k in range(n_dev):
            there = lax.rem(owner + k, n_dev)
            rows = work[:QLEN, :]
            for s in range(1, pair_slots):
                hit = in_range(jnp.full((QLEN, HD), pairs_ref[s]), there)
                rows = jnp.where(hit, work[s * QLEN : (s + 1) * QLEN, :], rows)
            pack[k, :, columns(j, HD)] = rows.astype(jnp.bfloat16)

    def spun(values):
        cosine = jnp.concatenate([turn[0, PLEN : PLEN + QLEN, :]] * pair_slots, axis=0)
        sine = jnp.concatenate([turn[1, PLEN : PLEN + QLEN, :]] * pair_slots, axis=0)
        return turned(values, cosine, sine)

    def suffix_queries(j, carry):
        raw_ = jnp.dot(suffix[...], wq[:, columns(j, HD)], preferred_element_type=jnp.float32)
        work[...] = spun(raw_) * HD ** (-0.5)
        store(j)
        return carry

    def suffix_keys(j, carry):
        raw_ = jnp.dot(suffix[...], wk[:, columns(j, HD)], preferred_element_type=jnp.float32)
        work[...] = spun(raw_)
        store(heads_q + j)
        return carry

    def suffix_values(j, carry):
        work[...] = jnp.dot(suffix[...], wv[:, columns(j, HD)], preferred_element_type=jnp.float32)
        store(heads_q + heads_kv + j)
        return carry

    lax.fori_loop(0, heads_q, suffix_queries, 0)
    lax.fori_loop(0, heads_kv, suffix_keys, 0)
    lax.fori_loop(0, heads_kv, suffix_values, 0)
    for k in range(1, n_dev):
        there = lax.rem(owner + k, n_dev)
        send(pack.at[k], received.at[k - 1], pair_send.at[k - 1], pair_recv.at[k - 1], "dev", there)

    for c in range(CHUNKS):
        at = pl.ds(c * unit, unit)
        arrived(passage.at[twin, at], rows_recv.at[twin, c])
    project(twin, 0, block_rows)
    for k in range(1, n_chips):
        here = peer(k)
        other = lax.rem(chip + k, n_chips) * 2 + 1 - core

        def step(many, i, carry):
            for part in range(many):
                c = i * many + part
                rows = passage.at[here, pl.ds(pl.multiple_of(c * unit, unit), unit)]
                arrived(rows, rows_recv.at[here, c])
                send(rows, rows, pass_send.at[k - 1, c], rows_recv.at[here, c], "tp", twin)
            first = pl.multiple_of(i * many * unit, many * unit)
            project(here, first, many * unit)
            for part in range(many):
                c = i * many + part
                rows = passage.at[other, pl.ds(pl.multiple_of(c * unit, unit), unit)]
                arrived(rows, rows_recv.at[other, c])
            project(other, first, many * unit)
            return carry

        lax.fori_loop(0, CHUNKS // 2 - 1, functools.partial(step, 2), 0)
        if halves:
            lax.fori_loop(CHUNKS - 2, CHUNKS - 1, functools.partial(step, 1), 0)

            def early_step(i, carry):
                arrived(received.at[i], pair_recv.at[i])
                attend(received.at[i], held, early.at[i + 1], heads_q, heads_kv, [chip])
                return carry

            attend(pack.at[0], held, early.at[0], heads_q, heads_kv, [chip])
            lax.fori_loop(0, n_dev - 1, early_step, 0)
            lax.fori_loop(CHUNKS - 1, CHUNKS, functools.partial(step, 1), 0)
        else:
            lax.fori_loop(CHUNKS - 2, CHUNKS, functools.partial(step, 1), 0)

    passages = [1 - chip] if halves else list(range(per_owner))

    def pair_step(i, carry):
        if not halves:
            arrived(received.at[i], pair_recv.at[i])
        other = early.at[i + 1] if halves else None
        attend(received.at[i], held, mixed.at[i], heads_q, heads_kv, passages, other)
        back = lax.rem(owner + n_dev - 1 - i, n_dev)
        send(mixed.at[i], returned.at[i + 1], back_send.at[i], back_recv.at[i], "dev", back)
        return carry

    lax.fori_loop(0, n_dev - 1, pair_step, 0)
    other = early.at[0] if halves else None
    attend(pack.at[0], held, returned.at[0], heads_q, heads_kv, passages, other)
    loads[5].wait()
    for i in range(n_dev - 1):
        arrived(returned.at[i + 1], back_recv.at[i])
    for s in range(pair_slots):
        name = jnp.full(returned.shape[1:], pairs_ref[s])
        rows = returned[0].astype(jnp.float32)
        for k in range(1, n_dev):
            there = lax.rem(owner + k, n_dev)
            rows = jnp.where(in_range(name, there), returned[k].astype(jnp.float32), rows)
        attended[s * QLEN : (s + 1) * QLEN, :] = rows.astype(jnp.bfloat16)

    def pass_on(j):
        arrived(twin_in.at[j], give_recv.at[j])
        summed = keep[j].astype(jnp.float32) + twin_in[j].astype(jnp.float32)
        merged[j] = summed[:size]
        for k in range(1, n_chips):
            sums[k - 1, j] = summed[k * size : (k + 1) * size].astype(jnp.bfloat16)
            send(
                sums.at[k - 1, j], sums_in.at[k - 1, j],
                sum_send.at[k - 1, j], sum_recv.at[k - 1, j], "tp", peer(k),
            )

    def out_step(j, carry):
        product[...] = jnp.dot(
            attended[...], wo[:, columns(j, TILE)], preferred_element_type=jnp.float32
        )
        for k in range(n_chips):
            base = lax.rem(chip + k, n_chips) * 2
            mine = pl.multiple_of((base + core) * size, size)
            theirs = pl.multiple_of((base + 1 - core) * size, size)
            at = pl.ds(k * size, size)
            keep[j, at, :] = product[pl.ds(mine, size), :].astype(jnp.bfloat16)
            give[j, at, :] = product[pl.ds(theirs, size), :].astype(jnp.bfloat16)
        send(give.at[j], twin_in.at[j], give_send.at[j], give_recv.at[j], "tp", twin)

        @pl.when(j > 0)
        def _():
            pass_on(j - 1)

        return carry

    lax.fori_loop(0, n_cols, out_step, 0)
    pass_on(n_cols - 1)
    squares = jnp.zeros((size, 1), jnp.float32)
    for j in range(n_cols):
        total = merged[j]
        for k in range(1, n_chips):
            arrived(sums_in.at[k - 1, j], sum_recv.at[k - 1, j])
            total = total + sums_in[k - 1, j].astype(jnp.float32)
        merged[j] = total
        squares = squares + jnp.sum(total * total, axis=1, keepdims=True)
    scale = lax.rsqrt(squares / width + epsilon)
    row_ids = lane * size + lax.broadcasted_iota(jnp.int32, (size, TILE), 0)
    alive = row_ids < count_ref[0] * QLEN
    for j in range(n_cols):
        at = slice(j * TILE, (j + 1) * TILE)
        branch = merged[j] * scale * gain_out_ref[at].astype(jnp.float32).reshape(1, TILE)
        whole = gathered[lane, :, at].astype(jnp.float32) + branch
        out_ref[:, at] = jnp.where(alive, whole, 0.0).astype(jnp.bfloat16)

    for k in range(2 * n_chips - 1):
        sent(gathered.at[0], query_send.at[k])
    for c in range(CHUNKS):
        rows = passage.at[0, pl.ds(0, unit)]
        sent(rows, near_send.at[c])
        for k in range(n_chips - 1):
            sent(rows, far_send.at[k, c])
            sent(rows, pass_send.at[k, c])
    for i in range(n_dev - 1):
        sent(received.at[i], pair_send.at[i])
        sent(mixed.at[i], back_send.at[i])
    for j in range(n_cols):
        sent(give.at[j], give_send.at[j])
        for k in range(n_chips - 1):
            sent(sums.at[k, j], sum_send.at[k, j])


def shards(
    passage_hidden,
    query_hidden,
    gain_in,
    gain_out,
    w_query,
    w_key,
    w_value,
    w_out,
    pair_passage,
    pair_count,
):
    n_tp, n_dev = lax.axis_size("tp"), lax.axis_size("dev")
    n_chips = n_tp // 2
    pair_slots = pair_passage.shape[0]
    block_rows, width = passage_hidden.shape
    size = query_hidden.shape[0]
    rows = pair_slots * QLEN
    wide_q, wide_kv = w_query.shape[1], w_key.shape[1]
    pack_width = wide_q + 2 * wide_kv + FLAG
    n_cols = width // TILE
    half = rows // 2
    bf, f32, dma = jnp.bfloat16, jnp.float32, pltpu.SemaphoreType.DMA
    smem = pl.BlockSpec(memory_space=pltpu.SMEM)
    vmem = pl.BlockSpec(memory_space=pltpu.VMEM)
    hbm = pl.BlockSpec(memory_space=pl.ANY)
    far = n_chips - 1
    return pl.pallas_call(
        functools.partial(body, n_tp, n_dev),
        out_shape=jax.ShapeDtypeStruct((size, width), bf),
        in_specs=[smem, smem, vmem, vmem] + [hbm] * 7,
        out_specs=vmem,
        scratch_shapes=[
            pltpu.VMEM((block_rows, width), bf),
            pltpu.VMEM((n_tp, block_rows, width), bf),
            pltpu.VMEM((n_tp * block_rows, 2 * wide_kv), bf),
            pltpu.VMEM((n_tp, size, width), bf),
            pltpu.VMEM((rows, width), bf),
            pltpu.VMEM((2, PLEN + QLEN, HALF), f32),
            pltpu.VMEM((n_dev, QLEN, pack_width), bf),
            pltpu.VMEM((n_dev - 1, QLEN, pack_width), bf),
            pltpu.VMEM((n_dev - 1, QLEN, wide_q), bf),
            pltpu.VMEM((n_dev, QLEN, wide_q), bf),
            pltpu.VMEM((n_dev, QLEN, wide_q), bf),
            pltpu.VMEM((rows, wide_q), bf),
            pltpu.VMEM(w_query.shape, bf),
            pltpu.VMEM(w_key.shape, bf),
            pltpu.VMEM(w_value.shape, bf),
            pltpu.VMEM(w_out.shape, bf),
            pltpu.VMEM((rows, HD), f32),
            pltpu.VMEM((rows, TILE), f32),
            pltpu.VMEM((n_cols, half, TILE), bf),
            pltpu.VMEM((n_cols, half, TILE), bf),
            pltpu.VMEM((n_cols, half, TILE), bf),
            pltpu.VMEM((far, n_cols, size, TILE), bf),
            pltpu.VMEM((far, n_cols, size, TILE), bf),
            pltpu.VMEM((n_cols, size, TILE), f32),
            dma((6,)),
            dma((CHUNKS,)),
            dma((2 * n_chips - 1,)),
            dma((n_tp,)),
            dma((CHUNKS,)),
            dma((far, CHUNKS)),
            dma((far, CHUNKS)),
            dma((n_tp, CHUNKS)),
            dma((n_dev - 1,)),
            dma((n_dev - 1,)),
            dma((n_dev - 1,)),
            dma((n_dev - 1,)),
            dma((n_cols,)),
            dma((n_cols,)),
            dma((far, n_cols)),
            dma((far, n_cols)),
        ],
        compiler_params=pltpu.CompilerParams(
            collective_id=0, has_side_effects=True, vmem_limit_bytes=VMEM_LIMIT
        ),
    )(
        pair_passage,
        pair_count,
        gain_in,
        gain_out,
        passage_hidden,
        query_hidden,
        tables(PLEN + QLEN),
        w_query,
        w_key,
        w_value,
        w_out,
    )


def solution(mesh):
    placed = (
        P(("grp", "dev", "tp"), None),
        P(("grp", "dev", "tp"), None),
        P(),
        P(),
        P(None, "tp"),
        P(None, "tp"),
        P(None, "tp"),
        P("tp", None),
        P(("grp", "dev")),
        P(("grp", "dev")),
    )
    return jax.shard_map(
        shards, mesh=mesh, in_specs=placed, out_specs=P(("grp", "dev", "tp"), None), check_vma=False
    )
```

```python
import functools

import jax
import jax.numpy as jnp
import numpy as np
from jax import lax
from jax.experimental import pallas as pl
from jax.experimental.pallas import tpu as pltpu
from jax.sharding import PartitionSpec as P

HD = 256
HALF = HD // 2
PLEN = 512
QLEN = 64
CHUNKS = 4
TILE = 512
FLAG = 128
VMEM_LIMIT = 56 * 1024 * 1024
MESH = pl.DeviceIdType.MESH

epsilon = 1e-06
softcap_limit = 50.0


def tables(count):
    frequency = (10000.0 ** (-2.0 * np.arange(HALF, dtype=np.float32) / HD)).astype(np.float32)
    positions = np.arange(count, dtype=np.float32)
    angles = (positions[:, None] * frequency[None, :]).astype(np.float32)
    return jnp.asarray(np.stack([np.cos(angles), np.sin(angles)]))


def normalize(rows, gain):
    values = rows.astype(jnp.float32)
    inverse_rms = lax.rsqrt(jnp.mean(values * values, axis=-1, keepdims=True) + epsilon)
    return (values * inverse_rms * gain).astype(jnp.bfloat16)


def turned(raw, cosine, sine):
    low, high = raw[:, :HALF], raw[:, HALF:]
    return jnp.concatenate([low * cosine - high * sine, high * cosine + low * sine], axis=1)


def capped_exp(scores):
    return jnp.exp(softcap_limit * jnp.tanh(scores * (1.0 / softcap_limit)))


def columns(j, width):
    return pl.ds(pl.multiple_of(j * width, width), width)


def attend(pair_ref, held_ref, out_ref, heads_q, heads_kv, passages, other_ref=None):
    groups = heads_q // heads_kv
    over = (((1,), (1,)), ((), ()))
    rows = lax.rem(lax.broadcasted_iota(jnp.int32, (groups * QLEN, QLEN), 0), QLEN)
    causal = rows >= lax.broadcasted_iota(jnp.int32, (groups * QLEN, QLEN), 1)
    flag_at = (heads_q + 2 * heads_kv) * HD
    flag = pair_ref[:, flag_at : flag_at + FLAG].astype(jnp.float32)[:, :1]
    flag = jnp.concatenate([flag] * groups, axis=0)
    for h in range(heads_kv):
        query = jnp.concatenate(
            [pair_ref[:, (h * groups + g) * HD : (h * groups + g + 1) * HD] for g in range(groups)],
            axis=0,
        )
        key_at, value_at = (heads_q + h) * HD, (heads_q + heads_kv + h) * HD
        keys_own = pair_ref[:, key_at : key_at + HD]
        values_own = pair_ref[:, value_at : value_at + HD]
        far = None
        for i, p in enumerate(passages):
            keys = held_ref[columns(p, PLEN), h * HD : (h + 1) * HD]
            scores = lax.dot_general(query, keys, over, preferred_element_type=jnp.float32)
            far = scores if i == 0 else jnp.where(flag == jnp.float32(p), scores, far)
        far = capped_exp(far)
        near = capped_exp(
            lax.dot_general(query, keys_own, over, preferred_element_type=jnp.float32)
        )
        near = jnp.where(causal, near, 0.0)
        total = jnp.sum(far, axis=1, keepdims=True) + jnp.sum(near, axis=1, keepdims=True)
        inverse = 1.0 / total
        far = far * inverse
        near = (near * inverse).astype(jnp.bfloat16)
        mixed = jnp.dot(near, values_own, preferred_element_type=jnp.float32)
        for p in passages:
            at = (heads_kv + h) * HD
            values = held_ref[columns(p, PLEN), at : at + HD]
            weights = far if len(passages) == 1 else jnp.where(flag == jnp.float32(p), far, 0.0)
            weights = weights.astype(jnp.bfloat16)
            mixed = mixed + jnp.dot(weights, values, preferred_element_type=jnp.float32)
        for g in range(groups):
            at = (h * groups + g) * HD
            part = mixed[g * QLEN : (g + 1) * QLEN]
            if other_ref is not None:
                chosen = flag[:QLEN] == passages[0].astype(jnp.float32)
                part = jnp.where(chosen, part, other_ref[:, at : at + HD].astype(jnp.float32))
            out_ref[:, at : at + HD] = part.astype(jnp.bfloat16)


def body(
    n_tp, n_dev,
    pairs_ref, count_ref, gain_in_ref, gain_out_ref, passage_ref, query_ref, table_ref,
    wq_ref, wk_ref, wv_ref, wo_ref, out_ref,
    raw, passage, held, gathered, suffix, turn, pack, received, mixed, early, returned, attended,
    wq, wk, wv, wo, work, product, keep, give, twin_in, sums, sums_in, merged,
    load_sem, raw_sem, query_send, query_recv, near_send, far_send, pass_send, rows_recv,
    pair_send, pair_recv, back_send, back_recv, give_send, give_recv, sum_send, sum_recv,
):
    n_chips = n_tp // 2
    lane, owner = lax.axis_index("tp"), lax.axis_index("dev")
    chip, core = lane // 2, lane % 2
    twin = chip * 2 + 1 - core
    heads_q, heads_kv = wq.shape[1] // HD, wk.shape[1] // HD
    block_rows, width = raw.shape
    unit = block_rows // CHUNKS
    size = query_ref.shape[0]
    per_owner = block_rows * n_tp // PLEN
    pair_slots = pairs_ref.shape[0]
    n_cols = width // TILE
    halves = n_chips == 2 and per_owner == 2

    def peer(k):
        return lax.rem(chip + k, n_chips) * 2 + core

    def send(src, dst, send_sem, recv_sem, axis, target):
        copy = pltpu.make_async_remote_copy(
            src_ref=src, dst_ref=dst, send_sem=send_sem, recv_sem=recv_sem,
            device_id={axis: target}, device_id_type=MESH,
        )
        copy.start()

    def sent(ref, sem):
        pltpu.make_async_remote_copy(
            src_ref=ref, dst_ref=ref, send_sem=sem, recv_sem=sem,
            device_id={"tp": twin}, device_id_type=MESH,
        ).wait_send()

    def arrived(ref, sem):
        pltpu.make_async_remote_copy(
            src_ref=ref, dst_ref=ref, send_sem=sem, recv_sem=sem,
            device_id={"tp": twin}, device_id_type=MESH,
        ).wait_recv()

    def in_range(names, holder):
        return (names >= holder * per_owner) & (names < (holder + 1) * per_owner)

    for c in range(CHUNKS):
        at = pl.ds(c * unit, unit)
        pltpu.make_async_copy(passage_ref.at[at], raw.at[at], raw_sem.at[c]).start()
    loads = [
        pltpu.make_async_copy(query_ref, gathered.at[lane], load_sem.at[0]),
        pltpu.make_async_copy(table_ref, turn, load_sem.at[1]),
        pltpu.make_async_copy(wk_ref, wk, load_sem.at[2]),
        pltpu.make_async_copy(wv_ref, wv, load_sem.at[3]),
        pltpu.make_async_copy(wq_ref, wq, load_sem.at[4]),
        pltpu.make_async_copy(wo_ref, wo, load_sem.at[5]),
    ]
    for load in loads:
        load.start()

    barrier = pltpu.get_barrier_semaphore()
    pl.semaphore_signal(barrier, inc=1, device_id={"tp": twin}, device_id_type=MESH)
    for k in range(1, n_chips):
        pl.semaphore_signal(barrier, inc=1, device_id={"tp": peer(k)}, device_id_type=MESH)
    for k in range(1, n_dev):
        there = lax.rem(owner + k, n_dev)
        pl.semaphore_signal(barrier, inc=1, device_id={"dev": there}, device_id_type=MESH)
    pl.semaphore_wait(barrier, n_chips + n_dev - 1)

    for k in range(1, n_chips):
        send(query_ref, gathered.at[lane], query_send.at[k], query_recv.at[lane], "tp", peer(k))
    send(query_ref, gathered.at[lane], query_send.at[0], query_recv.at[lane], "tp", twin)

    def norm_chunk(c, carry):
        at = pl.ds(pl.multiple_of(c * unit, unit), unit)
        pltpu.make_async_copy(passage_ref.at[at], raw.at[at], raw_sem.at[c]).wait()
        passage[lane, at, :] = normalize(raw[at, :], gain_in_ref[...].astype(jnp.float32).reshape(1, width))
        mine = passage.at[lane, at]
        for k in range(1, n_chips):
            send(mine, mine, far_send.at[k - 1, c], rows_recv.at[lane, c], "tp", peer(k))
        send(mine, mine, near_send.at[c], rows_recv.at[lane, c], "tp", twin)
        return carry

    lax.fori_loop(0, CHUNKS, norm_chunk, 0)

    def project(blocks, first, rows):
        def product_of(weights):
            parts = [passage[block, pl.ds(first, rows), :] for block in blocks]
            whole = parts[0] if len(parts) == 1 else jnp.concatenate(parts, axis=0)
            whole = jnp.dot(whole, weights, preferred_element_type=jnp.float32)
            return [whole[n * rows : (n + 1) * rows] for n in range(len(blocks))]

        def keys(j, carry):
            for block, part in zip(blocks, product_of(wk[:, columns(j, HD)])):
                row = block * block_rows + first
                spot = pl.ds(pl.multiple_of(lax.rem(row, PLEN), rows), rows)
                held[pl.ds(pl.multiple_of(row, rows), rows), columns(j, HD)] = turned(
                    part, turn[0, spot, :], turn[1, spot, :]
                ).astype(jnp.bfloat16)
            return carry

        def values(j, carry):
            for block, part in zip(blocks, product_of(wv[:, columns(j, HD)])):
                place = pl.ds(pl.multiple_of(block * block_rows + first, rows), rows)
                held[place, columns(heads_kv + j, HD)] = part.astype(jnp.bfloat16)
            return carry

        lax.fori_loop(0, heads_kv, keys, 0)
        lax.fori_loop(0, heads_kv, values, 0)

    for load in loads[1:4]:
        load.wait()
    project([lane], 0, block_rows)

    for k in range(1, n_chips):
        arrived(gathered.at[peer(k)], query_recv.at[peer(k)])
        block = gathered.at[peer(k)]
        send(block, block, query_send.at[n_chips + k - 1], query_recv.at[peer(k)], "tp", twin)
    arrived(gathered.at[twin], query_recv.at[twin])
    for k in range(1, n_chips):
        other = lax.rem(chip + k, n_chips) * 2 + 1 - core
        arrived(gathered.at[other], query_recv.at[other])
    loads[0].wait()
    for i in range(n_tp):
        suffix[i * size : (i + 1) * size, :] = normalize(gathered[i], gain_in_ref[...].astype(jnp.float32).reshape(1, width))
    flag_at = (heads_q + 2 * heads_kv) * HD
    for k in range(n_dev):
        there = lax.rem(owner + k, n_dev)
        name = jnp.full((QLEN, FLAG), pairs_ref[0])
        for s in range(1, pair_slots):
            other = jnp.full((QLEN, FLAG), pairs_ref[s])
            name = jnp.where(in_range(other, there), other, name)
        flag = jnp.zeros((QLEN, FLAG), jnp.float32)
        for p in range(1, per_owner):
            for o in range(n_dev):
                flag = jnp.where(name == o * per_owner + p, float(p), flag)
        pack[k, :, flag_at : flag_at + FLAG] = flag.astype(jnp.bfloat16)
    loads[4].wait()

    def store(j):
        for k in range(n_dev):
            there = lax.rem(owner + k, n_dev)
            rows = work[:QLEN, :]
            for s in range(1, pair_slots):
                hit = in_range(jnp.full((QLEN, HD), pairs_ref[s]), there)
                rows = jnp.where(hit, work[s * QLEN : (s + 1) * QLEN, :], rows)
            pack[k, :, columns(j, HD)] = rows.astype(jnp.bfloat16)

    def spun(values):
        cosine = jnp.concatenate([turn[0, PLEN : PLEN + QLEN, :]] * pair_slots, axis=0)
        sine = jnp.concatenate([turn[1, PLEN : PLEN + QLEN, :]] * pair_slots, axis=0)
        return turned(values, cosine, sine)

    def suffix_queries(j, carry):
        raw_ = jnp.dot(suffix[...], wq[:, columns(j, HD)], preferred_element_type=jnp.float32)
        work[...] = spun(raw_) * HD ** (-0.5)
        store(j)
        return carry

    def suffix_keys(j, carry):
        raw_ = jnp.dot(suffix[...], wk[:, columns(j, HD)], preferred_element_type=jnp.float32)
        work[...] = spun(raw_)
        store(heads_q + j)
        return carry

    def suffix_values(j, carry):
        work[...] = jnp.dot(suffix[...], wv[:, columns(j, HD)], preferred_element_type=jnp.float32)
        store(heads_q + heads_kv + j)
        return carry

    lax.fori_loop(0, heads_q, suffix_queries, 0)
    lax.fori_loop(0, heads_kv, suffix_keys, 0)
    lax.fori_loop(0, heads_kv, suffix_values, 0)
    for k in range(1, n_dev):
        there = lax.rem(owner + k, n_dev)
        send(pack.at[k], received.at[k - 1], pair_send.at[k - 1], pair_recv.at[k - 1], "dev", there)

    for c in range(CHUNKS):
        at = pl.ds(c * unit, unit)
        arrived(passage.at[twin, at], rows_recv.at[twin, c])
    project([twin], 0, block_rows)
    for k in range(1, n_chips):
        here = peer(k)
        other = lax.rem(chip + k, n_chips) * 2 + 1 - core

        def step(many, i, carry):
            for part in range(many):
                c = i * many + part
                rows = passage.at[here, pl.ds(pl.multiple_of(c * unit, unit), unit)]
                arrived(rows, rows_recv.at[here, c])
                send(rows, rows, pass_send.at[k - 1, c], rows_recv.at[here, c], "tp", twin)
            first = pl.multiple_of(i * many * unit, many * unit)
            for part in range(many):
                c = i * many + part
                rows = passage.at[other, pl.ds(pl.multiple_of(c * unit, unit), unit)]
                arrived(rows, rows_recv.at[other, c])
            project([here, other], first, many * unit)
            return carry

        lax.fori_loop(0, CHUNKS // 2 - 1, functools.partial(step, 2), 0)
        if halves:
            lax.fori_loop(CHUNKS - 2, CHUNKS - 1, functools.partial(step, 1), 0)

            def early_step(i, carry):
                arrived(received.at[i], pair_recv.at[i])
                attend(received.at[i], held, early.at[i + 1], heads_q, heads_kv, [chip])
                return carry

            attend(pack.at[0], held, early.at[0], heads_q, heads_kv, [chip])
            lax.fori_loop(0, n_dev - 1, early_step, 0)
            lax.fori_loop(CHUNKS - 1, CHUNKS, functools.partial(step, 1), 0)
        else:
            lax.fori_loop(CHUNKS - 2, CHUNKS, functools.partial(step, 1), 0)

    passages = [1 - chip] if halves else list(range(per_owner))

    def pair_step(i, carry):
        if not halves:
            arrived(received.at[i], pair_recv.at[i])
        other = early.at[i + 1] if halves else None
        attend(received.at[i], held, mixed.at[i], heads_q, heads_kv, passages, other)
        back = lax.rem(owner + n_dev - 1 - i, n_dev)
        send(mixed.at[i], returned.at[i + 1], back_send.at[i], back_recv.at[i], "dev", back)
        return carry

    lax.fori_loop(0, n_dev - 1, pair_step, 0)
    other = early.at[0] if halves else None
    attend(pack.at[0], held, returned.at[0], heads_q, heads_kv, passages, other)
    loads[5].wait()
    for i in range(n_dev - 1):
        arrived(returned.at[i + 1], back_recv.at[i])
    for s in range(pair_slots):
        name = jnp.full(returned.shape[1:], pairs_ref[s])
        rows = returned[0].astype(jnp.float32)
        for k in range(1, n_dev):
            there = lax.rem(owner + k, n_dev)
            rows = jnp.where(in_range(name, there), returned[k].astype(jnp.float32), rows)
        attended[s * QLEN : (s + 1) * QLEN, :] = rows.astype(jnp.bfloat16)

    def pass_on(j):
        arrived(twin_in.at[j], give_recv.at[j])
        summed = keep[j].astype(jnp.float32) + twin_in[j].astype(jnp.float32)
        merged[j] = summed[:size]
        for k in range(1, n_chips):
            sums[k - 1, j] = summed[k * size : (k + 1) * size].astype(jnp.bfloat16)
            send(
                sums.at[k - 1, j], sums_in.at[k - 1, j],
                sum_send.at[k - 1, j], sum_recv.at[k - 1, j], "tp", peer(k),
            )

    def out_step(j, carry):
        product[...] = jnp.dot(
            attended[...], wo[:, columns(j, TILE)], preferred_element_type=jnp.float32
        )
        for k in range(n_chips):
            base = lax.rem(chip + k, n_chips) * 2
            mine = pl.multiple_of((base + core) * size, size)
            theirs = pl.multiple_of((base + 1 - core) * size, size)
            at = pl.ds(k * size, size)
            keep[j, at, :] = product[pl.ds(mine, size), :].astype(jnp.bfloat16)
            give[j, at, :] = product[pl.ds(theirs, size), :].astype(jnp.bfloat16)
        send(give.at[j], twin_in.at[j], give_send.at[j], give_recv.at[j], "tp", twin)

        @pl.when(j > 0)
        def _():
            pass_on(j - 1)

        return carry

    lax.fori_loop(0, n_cols, out_step, 0)
    pass_on(n_cols - 1)
    squares = jnp.zeros((size, 1), jnp.float32)
    for j in range(n_cols):
        total = merged[j]
        for k in range(1, n_chips):
            arrived(sums_in.at[k - 1, j], sum_recv.at[k - 1, j])
            total = total + sums_in[k - 1, j].astype(jnp.float32)
        merged[j] = total
        squares = squares + jnp.sum(total * total, axis=1, keepdims=True)
    scale = lax.rsqrt(squares / width + epsilon)
    row_ids = lane * size + lax.broadcasted_iota(jnp.int32, (size, TILE), 0)
    alive = row_ids < count_ref[0] * QLEN
    for j in range(n_cols):
        at = slice(j * TILE, (j + 1) * TILE)
        branch = merged[j] * scale * gain_out_ref[at].astype(jnp.float32).reshape(1, TILE)
        whole = gathered[lane, :, at].astype(jnp.float32) + branch
        out_ref[:, at] = jnp.where(alive, whole, 0.0).astype(jnp.bfloat16)

    for k in range(2 * n_chips - 1):
        sent(gathered.at[0], query_send.at[k])
    for c in range(CHUNKS):
        rows = passage.at[0, pl.ds(0, unit)]
        sent(rows, near_send.at[c])
        for k in range(n_chips - 1):
            sent(rows, far_send.at[k, c])
            sent(rows, pass_send.at[k, c])
    for i in range(n_dev - 1):
        sent(received.at[i], pair_send.at[i])
        sent(mixed.at[i], back_send.at[i])
    for j in range(n_cols):
        sent(give.at[j], give_send.at[j])
        for k in range(n_chips - 1):
            sent(sums.at[k, j], sum_send.at[k, j])


def shards(
    passage_hidden,
    query_hidden,
    gain_in,
    gain_out,
    w_query,
    w_key,
    w_value,
    w_out,
    pair_passage,
    pair_count,
):
    n_tp, n_dev = lax.axis_size("tp"), lax.axis_size("dev")
    n_chips = n_tp // 2
    pair_slots = pair_passage.shape[0]
    block_rows, width = passage_hidden.shape
    size = query_hidden.shape[0]
    rows = pair_slots * QLEN
    wide_q, wide_kv = w_query.shape[1], w_key.shape[1]
    pack_width = wide_q + 2 * wide_kv + FLAG
    n_cols = width // TILE
    half = rows // 2
    bf, f32, dma = jnp.bfloat16, jnp.float32, pltpu.SemaphoreType.DMA
    smem = pl.BlockSpec(memory_space=pltpu.SMEM)
    vmem = pl.BlockSpec(memory_space=pltpu.VMEM)
    hbm = pl.BlockSpec(memory_space=pl.ANY)
    far = n_chips - 1
    return pl.pallas_call(
        functools.partial(body, n_tp, n_dev),
        out_shape=jax.ShapeDtypeStruct((size, width), bf),
        in_specs=[smem, smem, vmem, vmem] + [hbm] * 7,
        out_specs=vmem,
        scratch_shapes=[
            pltpu.VMEM((block_rows, width), bf),
            pltpu.VMEM((n_tp, block_rows, width), bf),
            pltpu.VMEM((n_tp * block_rows, 2 * wide_kv), bf),
            pltpu.VMEM((n_tp, size, width), bf),
            pltpu.VMEM((rows, width), bf),
            pltpu.VMEM((2, PLEN + QLEN, HALF), f32),
            pltpu.VMEM((n_dev, QLEN, pack_width), bf),
            pltpu.VMEM((n_dev - 1, QLEN, pack_width), bf),
            pltpu.VMEM((n_dev - 1, QLEN, wide_q), bf),
            pltpu.VMEM((n_dev, QLEN, wide_q), bf),
            pltpu.VMEM((n_dev, QLEN, wide_q), bf),
            pltpu.VMEM((rows, wide_q), bf),
            pltpu.VMEM(w_query.shape, bf),
            pltpu.VMEM(w_key.shape, bf),
            pltpu.VMEM(w_value.shape, bf),
            pltpu.VMEM(w_out.shape, bf),
            pltpu.VMEM((rows, HD), f32),
            pltpu.VMEM((rows, TILE), f32),
            pltpu.VMEM((n_cols, half, TILE), bf),
            pltpu.VMEM((n_cols, half, TILE), bf),
            pltpu.VMEM((n_cols, half, TILE), bf),
            pltpu.VMEM((far, n_cols, size, TILE), bf),
            pltpu.VMEM((far, n_cols, size, TILE), bf),
            pltpu.VMEM((n_cols, size, TILE), f32),
            dma((6,)),
            dma((CHUNKS,)),
            dma((2 * n_chips - 1,)),
            dma((n_tp,)),
            dma((CHUNKS,)),
            dma((far, CHUNKS)),
            dma((far, CHUNKS)),
            dma((n_tp, CHUNKS)),
            dma((n_dev - 1,)),
            dma((n_dev - 1,)),
            dma((n_dev - 1,)),
            dma((n_dev - 1,)),
            dma((n_cols,)),
            dma((n_cols,)),
            dma((far, n_cols)),
            dma((far, n_cols)),
        ],
        compiler_params=pltpu.CompilerParams(
            collective_id=0, has_side_effects=True, vmem_limit_bytes=VMEM_LIMIT
        ),
    )(
        pair_passage,
        pair_count,
        gain_in,
        gain_out,
        passage_hidden,
        query_hidden,
        tables(PLEN + QLEN),
        w_query,
        w_key,
        w_value,
        w_out,
    )


def solution(mesh):
    placed = (
        P(("grp", "dev", "tp"), None),
        P(("grp", "dev", "tp"), None),
        P(),
        P(),
        P(None, "tp"),
        P(None, "tp"),
        P(None, "tp"),
        P("tp", None),
        P(("grp", "dev")),
        P(("grp", "dev")),
    )
    return jax.shard_map(
        shards, mesh=mesh, in_specs=placed, out_specs=P(("grp", "dev", "tp"), None), check_vma=False
    )
```
